1024 devices in a mesh: expert: 16 (over x_hi, z), replica: 64 (over y, x_lo, core).
Axes of the slice: x: 8 (x_hi: 2, x_lo: 4; x = x_hi * 4 + x_lo), y: 8, z: 8, core: 2. Of those that a mesh axis runs over, the one named last changes fastest.
Arguments:
- tokens: bfloat16 [4096, 1280], P(('replica', 'expert')), may hold values from -6 to 6
- upstream: bfloat16 [4096, 1280], P(('replica', 'expert')), may hold values from -6 to 6
- experts: int32 [4096, 2], P('replica'), may hold values from 0 to 15, all different within a row; in each aligned block of 64 rows (0 to 63, 64 to 127, ...) at most 10 rows name the same one
- gates: float32 [4096, 2], P('replica'), may hold values from 0.1 to 1
- w_in: bfloat16 [16, 1280, 5120], P('expert', None, 'replica'), may hold values from -0.15625 to 0.15625
- w_out: bfloat16 [16, 5120, 1280], P('expert', 'replica'), may hold values from -0.078125 to 0.078125
Outputs:
- token_grads: bfloat16 [4096, 1280], P(('replica', 'expert'))
- grad_in: float32 [16, 1280, 5120], P('expert', None, 'replica')
- grad_out: float32 [16, 5120, 1280], P('expert', 'replica')
The draws below stay inside these ranges and needn't reach their ends.
Inputs may be any that keep to these rules, and one draw needn't show every extreme that they name: The two experts of a token differ. Among the 64 tokens of one group no expert is named more than 10 times, a bound that some block reaches; every expert is named somewhere.
All inputs are finite; a program needn't handle non-finite values.
Results may differ from the reference program's by a relative error of at most 0.0057.
Values may be sent and summed in bfloat16 or wider, within the bound.
A program may use at most 32 MiB of HBM per device.

```python
import math
import jax
import jax.numpy as jnp
import numpy as np
from jax import lax

D = 1280
FF = 5120
EXPERTS = 16
ROW_TOK = 64
C_ROW = 10
ROWS = 640
TOKENS = 4096
N_REPLICA = 64


def steps_of(rng, dims, pieces, least, largest):
    factor_of = 1.0
    for axis_at, blocks in pieces:
        heights = jax.random.uniform(jax.random.fold_in(jax.random.fold_in(rng, 6), axis_at), (blocks,), jnp.float32, least / len(pieces), largest / len(pieces))
        factor_of = factor_of * jnp.repeat(jnp.exp(heights), dims[axis_at] // blocks).reshape((-1,) + (1,) * (len(dims) - 1 - axis_at))
    return factor_of


def assign_block(own_key, own, number, rows, count, top, reach, lean):
    ranking = jax.random.permutation(own_key, count)
    crowded, common = portions_of(count, rows * top, reach, lean, True), portions_of(count, rows * top, reach, lean, False)
    places = jnp.arange(count)

    def named(tallies, offset_by):
        used = int((tallies > 0).sum())
        fixed = max(1, used // 4)
        moved = fixed + (places - fixed + offset_by * (used - fixed)) % max(1, count - fixed)
        return jnp.zeros((count,), jnp.int32).at[ranking[jnp.where(places < fixed, places, moved)]].set(jnp.asarray(tallies, jnp.int32))

    tallies = jnp.where(number % 4 == 0, named(crowded, number // 4), named(common, number - number // 4 - 1))
    mixed = jax.random.permutation(jax.random.fold_in(own, 3), count)
    donor, receiver = mixed[0:count // 2 * 2:2], mixed[1:count // 2 * 2:2]
    margin = jnp.minimum(tallies[donor] - 1, reach - tallies[receiver]) // 2
    margin = jnp.where((donor == ranking[0]) | (receiver == ranking[0]) | (tallies[receiver] == 0), 0, jnp.maximum(margin, 0))
    moved = jax.random.randint(jax.random.fold_in(own, 4), (count // 2,), 0, 1 << 20) % (margin + 1)
    tallies = tallies.at[donor].add(-moved).at[receiver].add(moved)
    labels = jnp.searchsorted(jnp.cumsum(tallies), jnp.arange(rows * top), side="right").astype(jnp.int32)
    table = labels.reshape(top, rows).T
    table = table[jax.random.permutation(jax.random.fold_in(own, 1), rows)]
    offset_by = jax.random.randint(jax.random.fold_in(own, 2), (rows, 1), 0, top)
    return jnp.take_along_axis(table, (jnp.arange(top)[None, :] + offset_by) % top, axis=1)


def portions_of(amount, total, bound, slope, full):
    loads = [(1 << 20) // math.isqrt(grade ** slope) + 1 for grade in range(1, amount + 1)]
    largest = bound if full else min(bound, max(-(-total // amount), total * loads[0] // sum(loads)))
    least = 1 if total - largest >= amount - 1 else 0
    holding, rest = [largest] + [least] * (amount - 1), total - largest - least * (amount - 1)
    while rest > 0:
        free = [i for i in range(1, amount) if holding[i] < largest] or [i for i in range(1, amount) if holding[i] < bound]
        pool, left = sum([loads[i] for i in free]), rest
        for i in free:
            addition = min(bound - holding[i], max(1, left * loads[i] // pool), rest)
            holding[i] = holding[i] + addition
            rest = rest - addition
    return np.array(holding)


def scatter_about(rng, extent, spread, bound, pieces=(), held_as=jnp.bfloat16):
    entries = jax.random.normal(rng, extent, jnp.float32) * spread
    if len(pieces) > 0:
        entries = steps_of(rng, extent, pieces, -0.22, 0.18) * entries
    return jnp.clip(entries, min=-bound, max=bound).astype(held_as)


def setup_inputs(seed: int = 0) -> dict:
    streams_of = jax.random.split(jax.random.key(seed), 7)
    tokens = scatter_about(streams_of[0], (TOKENS, D), 1.0, 6.0, ((0, 1024),))
    upstream = scatter_about(streams_of[1], (TOKENS, D), 1.0, 6.0, ((0, 1024),))
    experts_keys = jax.random.split(jax.random.fold_in(streams_of[2], 1), TOKENS // ROW_TOK)
    experts_turns = jax.random.permutation(jax.random.fold_in(streams_of[2], 3), TOKENS // ROW_TOK)
    experts = jax.vmap(lambda own, number: assign_block(jax.random.fold_in(streams_of[2], 2), own, number, ROW_TOK, EXPERTS, 2, C_ROW, 2))(experts_keys, experts_turns).reshape((TOKENS, 2))
    gates = jnp.clip(0.1 + 0.9 * jax.random.uniform(streams_of[3], (TOKENS, 2), jnp.float32) ** steps_of(streams_of[3], (TOKENS, 2), ((0, 64),), -0.2, 0.2), 0.1, 1.0)
    w_in = scatter_about(streams_of[4], (EXPERTS, D, FF), D ** -0.5, 0.15625, ((0, 16), (2, 64)))
    w_out = scatter_about(streams_of[5], (EXPERTS, FF, D), FF ** -0.5, 0.078125, ((0, 16), (1, 64)))
    return {"tokens": tokens, "upstream": upstream, "experts": experts, "gates": gates, "w_in": w_in, "w_out": w_out}


def reference(tokens, upstream, experts, gates, w_in, w_out):
    pairs = ROW_TOK * 2
    flat_ids = experts.reshape(N_REPLICA, pairs)
    onehot = (flat_ids[:, :, None] == jnp.arange(EXPERTS, dtype=jnp.int32)[None, None, :]).astype(jnp.int32)
    before = jnp.cumsum(onehot, axis=1) - onehot
    slot_pos = lax.optimization_barrier(jnp.sum(before * onehot, axis=2)).astype(jnp.int32)
    group_idx = jnp.broadcast_to(jnp.arange(N_REPLICA, dtype=jnp.int32)[:, None], flat_ids.shape)
    token_idx = (jnp.arange(TOKENS * 2, dtype=jnp.int32) // 2).reshape(N_REPLICA, pairs)
    gate_flat = gates.reshape(N_REPLICA, pairs)
    scaled = (gate_flat[:, :, None] * upstream[token_idx].astype(jnp.float32)).astype(jnp.bfloat16)
    slot_in = jnp.zeros((EXPERTS, N_REPLICA, C_ROW, D), jnp.bfloat16).at[flat_ids, group_idx, slot_pos].set(tokens[token_idx])
    slot_grad = jnp.zeros((EXPERTS, N_REPLICA, C_ROW, D), jnp.bfloat16).at[flat_ids, group_idx, slot_pos].set(scaled)
    slot_in = slot_in.reshape(EXPERTS, ROWS, D)
    slot_grad = slot_grad.reshape(EXPERTS, ROWS, D)

    def per_expert(items):
        inputs, grads, weight_in, weight_out = items
        pre = jnp.dot(inputs, weight_in, preferred_element_type=jnp.float32)
        act, back = jax.vjp(jax.nn.gelu, pre)
        dh = jnp.dot(grads, weight_out.T, preferred_element_type=jnp.float32)
        dpre = back(dh)[0].astype(jnp.bfloat16)
        grad_out_e = jnp.dot(act.astype(jnp.bfloat16).T, grads, preferred_element_type=jnp.float32)
        grad_in_e = jnp.dot(inputs.T, dpre, preferred_element_type=jnp.float32)
        slot_dx = jnp.dot(dpre, weight_in.T, preferred_element_type=jnp.float32)
        return (grad_in_e, grad_out_e, slot_dx)
    grad_in, grad_out, slot_dx = lax.map(per_expert, (slot_in, slot_grad, w_in, w_out))
    slot_dx = slot_dx.reshape(EXPERTS, N_REPLICA, C_ROW, D)
    picked = slot_dx[flat_ids, group_idx, slot_pos]
    token_grads = lax.optimization_barrier(jnp.sum(picked.reshape(TOKENS, 2, D), axis=1)).astype(jnp.bfloat16)
    return (token_grads, grad_in, grad_out)
```

```python
import functools

import jax
import jax.numpy as jnp
from jax import lax
from jax.experimental import pallas as pl
from jax.experimental.pallas import tpu as pltpu
from jax.sharding import PartitionSpec as P

MESH = pl.DeviceIdType.MESH
F32 = jnp.float32
BF16 = jnp.bfloat16
NZ, NH, NY, NX = 8, 2, 8, 4
NE = NZ * NH
SLOTS = 10
HALF = 640
GRP = NX * SLOTS
PLACE = {4: 0, 3: 1, 5: 2, 2: 3, 6: 4, 1: 5, 7: 6, 0: 7}


def iota(shape, dim):
    return lax.broadcasted_iota(jnp.int32, shape, dim)


def onehot(mask):
    return mask.astype(F32).astype(BF16)


def dot(a, b, dims=((1,), (0,))):
    return lax.dot_general(a, b, (dims, ((), ())), preferred_element_type=F32)


def tens(c):
    return (
        (c >= 10).astype(jnp.int32)
        + (c >= 20).astype(jnp.int32)
        + (c >= 30).astype(jnp.int32)
    )


def kernel(
    tok, up, ids, gates, w1, w2,
    out_tok, out_in, out_out,
    abuf, bbuf, X, G, W1, W2, dx, csend, crecv, vcat, psend, precv,
    dsend, drecv, gsend, grecv,
    a_send, a_recv, w_send, w_recv, b_send, b_recv, c_send, c_recv,
    p_send, p_recv, d_send, d_recv, g_send, g_recv,
):
    e = lax.axis_index("expert")
    r = lax.axis_index("replica")
    xh, z = e // NZ, e % NZ
    y, x, core = r // (NX * 2), (r // 2) % NX, r % 2

    def to_expert(e2):
        return {"expert": e2, "replica": r}

    def to_replica(y2, x2, c2):
        return {"expert": e, "replica": (y2 * NX + x2) * 2 + c2}

    twin = to_replica(y, x, 1 - core)
    y_up = to_replica((y + 1) % NY, x, core)
    y_dn = to_replica((y + NY - 1) % NY, x, core)
    x_peer = [None] + [to_replica(y, (x + d) % NX, core) for d in range(1, NX)]
    e_peer = [None] + [to_expert((e + d) % NE) for d in range(1, NE)]
    z_peer = [None] + [to_expert(xh * NZ + (z + d) % NZ) for d in range(1, NZ)]
    mirror = to_expert((1 - xh) * NZ + z)

    barrier = pltpu.get_barrier_semaphore()
    peers = [twin, y_up, y_dn] + x_peer[1:] + e_peer[1:]
    for peer in peers:
        pl.semaphore_signal(barrier, inc=1, device_id=peer, device_id_type=MESH)

    started = []

    def send(src, dst, s_sem, r_sem, peer):
        copy = pltpu.make_async_remote_copy(
            src_ref=src, dst_ref=dst, send_sem=s_sem, recv_sem=r_sem,
            device_id=peer, device_id_type=MESH,
        )
        copy.start()
        started.append(copy)

    def arrived(dst, r_sem, s_sem, peer):
        pltpu.make_async_remote_copy(
            src_ref=dst, dst_ref=dst, send_sem=s_sem, recv_sem=r_sem,
            device_id=peer, device_id_type=MESH,
        ).wait_recv()

    abuf[e] = jnp.concatenate(
        [
            tok[:, :HALF].astype(F32), tok[:, HALF:].astype(F32),
            up[:, :HALF].astype(F32), up[:, HALF:].astype(F32),
        ],
        axis=0,
    ).astype(BF16)
    W1[0:80] = w1[...]
    W2[0:80] = w2[...]
    pl.semaphore_wait(barrier, len(peers))

    own = abuf.at[e]
    send(own, own, a_send.at[0], a_recv.at[e], mirror)
    for d in (4, 3, 5, 2, 6, 1, 7):
        send(own, own, a_send.at[d], a_recv.at[e], z_peer[d])
    send(w1, W1.at[pl.ds(80, 80)], w_send.at[0], w_recv.at[0], twin)
    send(w2, W2.at[pl.ds(80, 80)], w_send.at[1], w_recv.at[1], twin)

    id0, id1 = ids[0:1, :], ids[1:2, :]
    hit0, hit1 = id0 == e, id1 == e
    chosen = (hit0 | hit1).astype(F32)
    gate = jnp.where(hit0, gates[0:1, :], jnp.where(hit1, gates[1:2, :], 0.0))
    ch8 = jnp.broadcast_to(chosen, (8, 64))
    tri = onehot(iota((64, 64), 0) < iota((64, 64), 1))
    v8 = jnp.where(ch8 > 0.5, dot(ch8.astype(BF16), tri), 99.0)
    c256 = iota((64, 256), 1)
    spread = onehot(iota((64, 256), 0) == (c256 >> 4) * 4 + (c256 & 3))
    vexp = dot(v8.astype(BF16), spread)[0:1, :]
    r40 = iota((GRP, 256), 0)
    part = tens(r40)
    slot = (r40 - 10 * part).astype(F32)
    col = iota((GRP, 256), 1)
    pick = onehot((vexp == slot) & (part == ((col >> 2) & 3)))
    slot64 = slot[:, 0:64]
    gcol = jnp.sum(jnp.where(v8[0:1, :] == slot64, gate, 0.0), axis=1, keepdims=True)
    gcol = jnp.where(part[:, 0:1] >= 2, gcol, 1.0)

    pe = (1 - xh) * NZ + z
    arrived(abuf.at[pe], a_recv.at[pe], a_send.at[0], mirror)
    for d in (4, 3, 5, 2, 6, 1, 7):
        send(abuf.at[pe], abuf.at[pe], a_send.at[NZ + d], a_recv.at[pe], z_peer[d])
    for h in range(2):
        for d in range(1, NZ):
            s = ((xh + h) % 2) * NZ + (z + d) % NZ
            arrived(abuf.at[s], a_recv.at[s], a_send.at[0], z_peer[d])
    rows = abuf[...].reshape(NE * 16, HALF)
    bbuf[y, x] = (dot(pick, rows) * gcol).astype(BF16)

    p160, c160 = iota((4 * GRP, GRP), 0), iota((4 * GRP, GRP), 1)
    perms = [onehot(p160 == c160 + 30 * tens(c160) + 10 * j) for j in range(NX)]

    def assemble(d):
        yy = (y + d) % NY
        m = dot(perms[0], bbuf[yy, 0])
        for j in range(1, NX):
            m = m + dot(perms[j], bbuf[yy, j])
        m = m.astype(BF16)
        at = PLACE[d] * GRP
        X[at:at + GRP, 0:HALF] = m[0:GRP]
        X[at:at + GRP, HALF:] = m[GRP:2 * GRP]
        G[at:at + GRP, 0:HALF] = m[2 * GRP:3 * GRP]
        G[at:at + GRP, HALF:] = m[3 * GRP:4 * GRP]

    mine = bbuf.at[y, x]
    b_at = [0]

    def b_go(yy, j, peer):
        ref = bbuf.at[yy, j]
        send(ref, ref, b_send.at[b_at[0]], b_recv.at[yy * NX + j], peer)
        b_at[0] += 1

    def b_in(yy, j, peer):
        arrived(bbuf.at[yy, j], b_recv.at[yy * NX + j], b_send.at[0], peer)

    b_go(y, x, y_up)
    b_go(y, x, y_dn)
    for d in (2, 1, 3):
        b_go(y, x, x_peer[d])
    for k in range(0, 5):
        for c in range(NX):
            j = (x + c) % NX
            n_up = 4 if c % 2 == 0 else 3
            n_dn = 7 - n_up
            if k == 0:
                if c > 0:
                    b_in(y, j, x_peer[c])
                    b_go(y, j, y_up)
                    b_go(y, j, y_dn)
                continue
            if k <= n_up:
                yy = (y + NY - k) % NY
                b_in(yy, j, y_dn)
                if k < n_up:
                    b_go(yy, j, y_up)
            if k <= n_dn:
                yy = (y + k) % NY
                b_in(yy, j, y_up)
                if k < n_dn:
                    b_go(yy, j, y_dn)
        assemble(k % NY)
        if 0 < k < 4:
            assemble(NY - k)

    arrived(W1.at[pl.ds(80, 80)], w_recv.at[0], w_send.at[0], twin)
    arrived(W2.at[pl.ds(80, 80)], w_recv.at[1], w_send.at[1], twin)

    last = ((1,), (1,))
    pre = dot(W1[...], X[...], last)
    dh = dot(W2[...], G[...], last)
    k0 = 0.7978845608028654
    sq = pre * pre
    t = jnp.tanh(k0 * (pre + 0.044715 * (sq * pre)))
    cdf = 0.5 * (1.0 + t)
    act = (pre * cdf).astype(BF16)
    slope = cdf + pre * (0.5 * (1.0 - t * t)) * (k0 * (1.0 + 3 * 0.044715 * sq))
    dpre32 = dh * slope
    dpre = dpre32.astype(BF16)
    dx[...] = dot(dpre32.T.astype(BF16), W1[...])

    def c_index(c, sign, k):
        return c * 7 + k + (0 if sign > 0 else (4 if c == 0 else 3))

    def c_step(k):
        for c in range(2):
            for sign in (1, -1):
                n = 4 if (c == 0) == (sign > 0) else 3
                if k >= n:
                    continue
                d = sign * (n - k)
                at = PLACE[d % NY] * GRP
                val = dx[at:at + GRP, c * HALF:(c + 1) * HALF]
                if k > 0:
                    i = c_index(c, sign, k - 1)
                    arrived(crecv.at[i], c_recv.at[i], c_send.at[i], y_dn if sign > 0 else y_up)
                    val = val + crecv[i].astype(F32)
                i = c_index(c, sign, k)
                csend[i] = val.astype(BF16)
                send(csend.at[i], crecv.at[i], c_send.at[i], c_recv.at[i], y_up if sign > 0 else y_dn)

    c_step(0)
    g_in = dot(dpre, X[...])
    out_in[...] = g_in[0:80]
    gsend[0] = g_in[80:160]
    send(gsend.at[0], grecv.at[0], g_send.at[0], g_recv.at[0], twin)
    c_step(1)
    g_out = dot(act, G[...])
    out_out[...] = g_out[0:80]
    gsend[1] = g_out[80:160]
    send(gsend.at[1], grecv.at[1], g_send.at[1], g_recv.at[1], twin)
    c_step(2)
    c_step(3)
    for c in range(2):
        at = PLACE[0] * GRP
        val = dx[at:at + GRP, c * HALF:(c + 1) * HALF]
        for sign in (1, -1):
            n = 4 if (c == 0) == (sign > 0) else 3
            i = c_index(c, sign, n - 1)
            arrived(crecv.at[i], c_recv.at[i], c_send.at[i], y_dn if sign > 0 else y_up)
            val = val + crecv[i].astype(F32)
        vcat[c * GRP:(c + 1) * GRP] = val.astype(BF16)

    q_row, q_col = iota((24, 2 * GRP), 0), iota((24, 2 * GRP), 1)
    q_half = (q_row >= 10).astype(jnp.int32)
    q_at = jnp.where(q_row < 20, q_half * 30 + q_row, -1000)
    sums = vcat[...]
    for d in (2, 1, 3):
        j = (x + d) % NX
        psend[d - 1] = dot(onehot(q_col == q_at + 10 * j), sums).astype(BF16)
        send(psend.at[d - 1], precv.at[d - 1], p_send.at[d - 1], p_recv.at[d - 1], x_peer[d])
    total = dot(onehot(q_col == q_at + 10 * x), sums)

    r64 = iota((128, 64), 0)
    gather = onehot(iota((128, 64), 1) == (r64 >> 3) * 4 + (r64 & 3))
    v_row = dot(gather, v8.astype(BF16), last)[:, 0:1]
    t_row, t_col = iota((128, 24), 0), iota((128, 24), 1)
    t_half = (t_col >= 10).astype(jnp.int32)
    t_slot = jnp.where(t_col < 20, t_col - 10 * t_half, 50).astype(F32)
    back = onehot((v_row == t_slot) & (((t_row >> 2) & 1) == t_half))

    for d in (1, 3, 2):
        arrived(precv.at[d - 1], p_recv.at[d - 1], p_send.at[d - 1], x_peer[NX - d])
        total = total + precv[d - 1].astype(F32)
    spread_rows = dot(back, total.astype(BF16))
    dsend[...] = spread_rows.reshape(NE, 8, HALF).astype(BF16)
    for d in (8, 12, 4, 9, 7, 10, 6, 11, 5, 13, 3, 14, 2, 15, 1):
        send(dsend.at[(e + d) % NE], drecv.at[d - 1], d_send.at[d - 1], d_recv.at[d - 1], e_peer[d])

    for i, out in ((0, out_in), (1, out_out)):
        arrived(grecv.at[i], g_recv.at[i], g_send.at[i], twin)
        out[...] = out[...] + grecv[i]

    res = dsend[e].astype(F32)
    for d in range(1, NE):
        arrived(drecv.at[d - 1], d_recv.at[d - 1], d_send.at[d - 1], e_peer[NE - d])
        res = res + drecv[d - 1].astype(F32)
    out_tok[:, :HALF] = res[0:4].astype(BF16)
    out_tok[:, HALF:] = res[4:8].astype(BF16)

    for copy in started:
        copy.wait_send()


def local(tokens, upstream, experts, gates, w_in, w_out):
    vmem = pl.BlockSpec(memory_space=pltpu.VMEM)
    dma = pltpu.SemaphoreType.DMA
    rows = NY * GRP
    width = 2 * HALF
    out_tok, out_in, out_out = pl.pallas_call(
        kernel,
        out_shape=(
            jax.ShapeDtypeStruct((4, width), BF16),
            jax.ShapeDtypeStruct((80, width), F32),
            jax.ShapeDtypeStruct((80, width), F32),
        ),
        in_specs=[vmem] * 6,
        out_specs=(vmem, vmem, vmem),
        scratch_shapes=[
            pltpu.VMEM((NE, 16, HALF), BF16),
            pltpu.VMEM((NY, NX, GRP, HALF), BF16),
            pltpu.VMEM((rows, width), BF16),
            pltpu.VMEM((rows, width), BF16),
            pltpu.VMEM((160, width), BF16),
            pltpu.VMEM((160, width), BF16),
            pltpu.VMEM((rows, width), F32),
            pltpu.VMEM((14, GRP, HALF), BF16),
            pltpu.VMEM((14, GRP, HALF), BF16),
            pltpu.VMEM((2 * GRP, HALF), BF16),
            pltpu.VMEM((3, 24, HALF), BF16),
            pltpu.VMEM((3, 24, HALF), BF16),
            pltpu.VMEM((NE, 8, HALF), BF16),
            pltpu.VMEM((NE - 1, 8, HALF), BF16),
            pltpu.VMEM((2, 80, width), F32),
            pltpu.VMEM((2, 80, width), F32),
            dma((NE,)), dma((NE,)), dma((2,)), dma((2,)), dma((31,)), dma((32,)),
            dma((14,)), dma((14,)), dma((3,)), dma((3,)), dma((15,)), dma((15,)),
            dma((2,)), dma((2,)),
        ],
        compiler_params=pltpu.CompilerParams(
            collective_id=0, has_side_effects=True, vmem_limit_bytes=40 * 1024 * 1024
        ),
        cost_estimate=pl.CostEstimate(flops=700_000_000, bytes_accessed=2_000_000, transcendentals=51200),
        name="moe_backward",
    )(tokens, upstream, experts.T, gates.T, w_in[0].T, w_out[0])
    return out_tok, out_in.T[None], out_out[None]


def solution(mesh):
    in_specs = (
        P(("replica", "expert"), None),
        P(("replica", "expert"), None),
        P("replica", None),
        P("replica", None),
        P("expert", None, "replica"),
        P("expert", "replica", None),
    )
    out_specs = (
        P(("replica", "expert"), None),
        P("expert", None, "replica"),
        P("expert", "replica", None),
    )
    return jax.shard_map(local, mesh=mesh, in_specs=in_specs, out_specs=out_specs, check_vma=False)
```

```python
import functools

import jax
import jax.numpy as jnp
from jax import lax
from jax.experimental import pallas as pl
from jax.experimental.pallas import tpu as pltpu
from jax.sharding import PartitionSpec as P

MESH = pl.DeviceIdType.MESH
F32 = jnp.float32
BF16 = jnp.bfloat16
NZ, NH, NY, NX = 8, 2, 8, 4
NE = NZ * NH
HALF = 640


def iota(shape, dim):
    return lax.broadcasted_iota(jnp.int32, shape, dim)


def onehot(mask):
    return mask.astype(F32).astype(BF16)


def dot(a, b, dims=((1,), (0,))):
    return lax.dot_general(a, b, (dims, ((), ())), preferred_element_type=F32)


def kernel(
    tok_hbm, up_hbm, ids_hbm, gates_hbm, w1, w2,
    out_tok, out_in, out_out,
    tok, up, ids, gates,
    abuf, bbuf, X, G, W1, W2, dx, csend, crecv,
    dsend, drecv, gtwin, gfrom, gsend, grecv,
    load_sem, a_send, a_recv, w_send, w_recv, b_send, b_recv, c_send, c_recv,
    d_send, d_recv, t_send, t_recv, g_send, g_recv,
):
    e = lax.axis_index("expert")
    r = lax.axis_index("replica")
    xh, z = e // NZ, e % NZ
    y, x, core = r // (NX * 2), (r // 2) % NX, r % 2

    def to_expert(e2):
        return {"expert": e2, "replica": r}

    def to_replica(y2, x2, c2):
        return {"expert": e, "replica": (y2 * NX + x2) * 2 + c2}

    twin = to_replica(y, x, 1 - core)
    home = (y % 2) * 2 + x % 2
    column = [home, home + 1 - 2 * (home % 2), (home + 2) % 4, 3 - home]
    x_flip, y_flip = x + 1 - 2 * (x % 2), y + 1 - 2 * (y % 2)
    chip_peer = [None, to_replica(y, x_flip, core), to_replica(y_flip, x, core), to_replica(y_flip, x_flip, core)]
    def place(d):
        return (y + 2 * (d // 2)) % NY, (x + 2 * (d % 2)) % NX

    def number(d):
        y2, x2 = place(d)
        return (y2 // 2) * 2 + x2 // 2

    group_peer = [None] + [to_replica(*place(d), core) for d in range(1, NY)]
    seen = [0] + [((4 - d // 2) % 4) * 2 + d % 2 for d in range(1, NY)]
    this = number(0)
    e_peer = [None] + [to_expert((e + d) % NE) for d in range(1, NE)]
    z_peer = [None] + [to_expert(xh * NZ + (z + d) % NZ) for d in range(1, NZ)]
    mirror = to_expert((1 - xh) * NZ + z)
    far_first = (4, 3, 5, 2, 6, 1, 7)
    groups_first = (5, 3, 7, 4, 1, 2, 6)

    barrier = pltpu.get_barrier_semaphore()
    peers = [twin] + group_peer[1:] + chip_peer[1:] + e_peer[1:]
    for peer in peers:
        pl.semaphore_signal(barrier, inc=1, device_id=peer, device_id_type=MESH)

    me = home * 2 + core
    loads = [
        pltpu.make_async_copy(src, dst, load_sem.at[i])
        for i, (src, dst) in enumerate(
            (
                (tok_hbm, tok), (up_hbm, up), (ids_hbm, ids), (gates_hbm, gates),
                (w1, W1.at[me]), (w2, W2.at[me]),
            )
        )
    ]
    for load in loads:
        load.start()
    started = []

    def send(src, dst, s_sem, r_sem, peer):
        copy = pltpu.make_async_remote_copy(
            src_ref=src, dst_ref=dst, send_sem=s_sem, recv_sem=r_sem,
            device_id=peer, device_id_type=MESH,
        )
        copy.start()
        started.append(copy)

    def arrived(dst, r_sem, s_sem, peer):
        pltpu.make_async_remote_copy(
            src_ref=dst, dst_ref=dst, send_sem=s_sem, recv_sem=r_sem,
            device_id=peer, device_id_type=MESH,
        ).wait_recv()

    loads[0].wait()
    loads[1].wait()
    abuf[e] = jnp.concatenate(
        [
            tok[:, :HALF].astype(F32), tok[:, HALF:].astype(F32),
            up[:, :HALF].astype(F32), up[:, HALF:].astype(F32),
        ],
        axis=0,
    ).astype(BF16)
    pl.semaphore_wait(barrier, len(peers))

    own = abuf.at[e]
    send(own, own, a_send.at[0], a_recv.at[e], mirror)
    for d in far_first:
        send(own, own, a_send.at[d], a_recv.at[e], z_peer[d])
    loads[4].wait()
    loads[5].wait()
    weights = (W1, W2)

    def w_go(i, at, s_at, peer):
        ref = weights[i].at[at]
        send(ref, ref, w_send.at[i, s_at], w_recv.at[i, at], peer)

    def w_in(i, at, peer):
        arrived(weights[i].at[at], w_recv.at[i, at], w_send.at[i, 0], peer)

    w_go(0, me, 1, chip_peer[1])
    w_go(0, me, 2, chip_peer[2])
    w_go(0, me, 0, twin)
    w_go(1, me, 0, twin)

    loads[2].wait()
    loads[3].wait()
    id0, id1 = ids[0:1, :], ids[1:2, :]
    hit0, hit1 = id0 == e, id1 == e
    chosen = (hit0 | hit1).astype(F32)
    gate = jnp.where(hit0, gates[0:1, :], jnp.where(hit1, gates[1:2, :], 0.0))
    ch8 = jnp.broadcast_to(chosen, (8, 64))
    tri = onehot(iota((64, 64), 0) < iota((64, 64), 1))
    v8 = jnp.where(ch8 > 0.5, dot(ch8.astype(BF16), tri), 99.0)
    c256 = iota((64, 256), 1)
    spread = onehot(iota((64, 256), 0) == (c256 >> 4) * 4 + (c256 & 3))
    vexp = dot(v8.astype(BF16), spread)[0:1, :]
    r40 = iota((40, 256), 0)
    part = jnp.where(r40 < 32, r40 >> 3, (r40 >> 1) & 3)
    slot = jnp.where(r40 < 32, r40 & 7, 8 + (r40 & 1)).astype(F32)
    col = iota((40, 256), 1)
    pick = onehot((vexp == slot) & (part == ((col >> 2) & 3)))
    slot64 = slot[:, 0:64]
    gcol = jnp.sum(jnp.where(v8[0:1, :] == slot64, gate, 0.0), axis=1, keepdims=True)
    gcol = jnp.where(part[:, 0:1] >= 2, gcol, 1.0)

    pe = (1 - xh) * NZ + z
    arrived(abuf.at[pe], a_recv.at[pe], a_send.at[0], mirror)
    for d in far_first:
        send(abuf.at[pe], abuf.at[pe], a_send.at[NZ + d], a_recv.at[pe], z_peer[d])
    w_go(1, me, 1, chip_peer[1])
    w_go(1, me, 2, chip_peer[2])
    for h in range(2):
        for d in range(1, NZ):
            s = ((xh + h) % 2) * NZ + (z + d) % NZ
            arrived(abuf.at[s], a_recv.at[s], a_send.at[0], z_peer[d])
    rows = abuf[...].reshape(NE * 16, HALF)
    bbuf[this] = (dot(pick, rows) * gcol).astype(BF16)

    for d in groups_first:
        send(bbuf.at[this], bbuf.at[this], b_send.at[d], b_recv.at[this], group_peer[d])

    ats = [column[c] * 2 + core for c in range(4)]
    w_in(0, ats[1], chip_peer[1])
    w_go(0, ats[1], 3, chip_peer[2])
    w_in(1, ats[2], chip_peer[2])
    w_go(1, ats[2], 3, chip_peer[1])
    w_go(0, ats[1], 4, twin)
    w_go(1, ats[2], 4, twin)
    w_in(0, ats[2], chip_peer[2])
    w_go(0, ats[2], 5, twin)
    w_in(1, ats[1], chip_peer[1])
    w_go(1, ats[1], 5, twin)
    w_in(0, ats[3], chip_peer[2])
    w_go(0, ats[3], 6, twin)
    w_in(1, ats[3], chip_peer[1])
    w_go(1, ats[3], 6, twin)

    for d in range(1, NY):
        yy = number(d)
        arrived(bbuf.at[yy], b_recv.at[yy], b_send.at[0], group_peer[d])
    for yy in range(NY):
        for k, (out, lane) in enumerate(((X, 0), (X, HALF), (G, 0), (G, HALF))):
            out[yy * 8:yy * 8 + 8, lane:lane + HALF] = bbuf[yy, 8 * k:8 * k + 8]
    tails = jnp.concatenate([bbuf[yy, 32:40] for yy in range(NY)], axis=0)
    o64, i64 = iota((64, 64), 0), iota((64, 64), 1)
    order_tails = onehot(o64 == ((i64 >> 1) & 3) * 16 + (i64 >> 3) * 2 + (i64 & 1))
    tail = dot(order_tails, tails).astype(BF16)
    X[64:80, 0:HALF] = tail[0:16]
    X[64:80, HALF:] = tail[16:32]
    G[64:80, 0:HALF] = tail[32:48]
    G[64:80, HALF:] = tail[48:64]

    for c in range(NX):
        at = column[c] * 2 + 1 - core
        for i in range(2):
            w_in(i, at, twin)

    last = ((1,), (1,))
    hidden, width = NX * 2 * 80, 2 * HALF
    pre = dot(W1[...].reshape(hidden, width), X[...], last)
    dh = dot(W2[...].reshape(hidden, width), G[...], last)
    k0 = 0.7978845608028654
    sq = pre * pre
    t = jnp.tanh(k0 * (pre + 0.044715 * (sq * pre)))
    cdf = 0.5 * (1.0 + t)
    act = (pre * cdf).astype(BF16)
    slope = cdf + pre * (0.5 * (1.0 - t * t)) * (k0 * (1.0 + 3 * 0.044715 * sq))
    dpre32 = dh * slope
    dpre = dpre32.astype(BF16)
    dx[...] = dot(dpre32.T.astype(BF16), W1[...].reshape(hidden, width)).astype(BF16)

    q_row, q_col = iota((24, 80), 0), iota((24, 80), 1)

    def group_rows(half, yy):
        q_slot = q_row - 10 * half
        inside = (q_slot >= 0) & (q_slot < 10)
        source = jnp.where(q_slot < 8, yy * 8 + q_slot, 56 + yy * 2 + q_slot)
        return onehot(inside & (q_col == source))

    def piece(d):
        yy = number(d)
        return dot(group_rows(0, yy), dx[:, :HALF]) + dot(group_rows(1, yy), dx[:, HALF:])

    for d in groups_first:
        csend[d - 1] = piece(d).astype(BF16)
        send(csend.at[d - 1], crecv.at[d - 1], c_send.at[d - 1], c_recv.at[d - 1], group_peer[d])
    total = piece(0)

    for i, (left, right) in enumerate(((dpre, X), (act, G))):
        full = dot(left, right[...])
        for k in range(2 * NX):
            gtwin[i, k] = full[k * 80:(k + 1) * 80]
    for c in (3, 2, 1, 0):
        at = column[c] * 2 + 1 - core
        for i in range(2):
            send(gtwin.at[i, at], gfrom.at[i, column[c]], t_send.at[i, c], t_recv.at[i, column[c]], twin)

    def g_go(c, i):
        arrived(gfrom.at[i, column[c]], t_recv.at[i, column[c]], t_send.at[i, c], twin)
        both = gtwin[i, column[c] * 2 + core] + gfrom[i, column[c]]
        gsend[c - 1, i] = both.astype(BF16)
        send(gsend.at[c - 1, i], grecv.at[c - 1, i], g_send.at[c - 1, i], g_recv.at[c - 1, i], chip_peer[c])

    g_go(1, 0)
    g_go(2, 0)

    r64 = iota((128, 64), 0)
    gather = onehot(iota((128, 64), 1) == (r64 >> 3) * 4 + (r64 & 3))
    v_row = dot(gather, v8.astype(BF16), last)[:, 0:1]
    t_row, t_col = iota((128, 24), 0), iota((128, 24), 1)
    t_half = (t_col >= 10).astype(jnp.int32)
    t_slot = jnp.where(t_col < 20, t_col - 10 * t_half, 50).astype(F32)
    back = onehot((v_row == t_slot) & (((t_row >> 2) & 1) == t_half))

    for d in range(1, NY):
        arrived(crecv.at[d - 1], c_recv.at[d - 1], c_send.at[d - 1], group_peer[seen[d]])
        total = total + crecv[d - 1].astype(F32)
    spread_rows = dot(back, total.astype(BF16))
    dsend[...] = spread_rows.reshape(NE, 8, HALF).astype(BF16)
    for d in (8, 12, 4, 9, 7, 10, 6, 11, 5, 13, 3, 14, 2, 15, 1):
        pltpu.make_async_remote_copy(
            src_ref=dsend.at[(e + d) % NE], dst_ref=drecv.at[d - 1],
            send_sem=d_send, recv_sem=d_recv, device_id=e_peer[d], device_id_type=MESH,
        ).start()

    g_go(3, 0)
    g_go(3, 1)
    g_go(1, 1)
    g_go(2, 1)
    for i in range(2):
        arrived(gfrom.at[i, home], t_recv.at[i, home], t_send.at[i, 0], twin)
    landed = pltpu.make_async_remote_copy(
        src_ref=drecv, dst_ref=drecv, send_sem=d_send, recv_sem=d_recv,
        device_id=e_peer[1], device_id_type=MESH,
    )
    landed.wait_recv()
    res = dsend[e].astype(F32)
    for d in range(1, NE):
        res = res + drecv[d - 1].astype(F32)
    out_tok[:, :HALF] = res[0:4].astype(BF16)
    out_tok[:, HALF:] = res[4:8].astype(BF16)
    for c in (1, 2, 3):
        for i in range(2):
            arrived(grecv.at[c - 1, i], g_recv.at[c - 1, i], g_send.at[c - 1, i], chip_peer[c])
    for i, out in ((0, out_in), (1, out_out)):
        res = gtwin[i, me] + gfrom[i, home]
        for c in range(1, NX):
            res = res + grecv[c - 1, i].astype(F32)
        out[...] = res
    landed.wait_send()
    for copy in started:
        copy.wait_send()


def local(tokens, upstream, experts, gates, w_in, w_out):
    vmem = pl.BlockSpec(memory_space=pltpu.VMEM)
    dma = pltpu.SemaphoreType.DMA
    width = 2 * HALF
    out_tok, out_in, out_out = pl.pallas_call(
        kernel,
        out_shape=(
            jax.ShapeDtypeStruct((4, width), BF16),
            jax.ShapeDtypeStruct((80, width), F32),
            jax.ShapeDtypeStruct((80, width), F32),
        ),
        in_specs=[pl.BlockSpec(memory_space=pltpu.HBM)] * 6,
        out_specs=(vmem, vmem, vmem),
        scratch_shapes=[
            pltpu.VMEM((4, width), BF16),
            pltpu.VMEM((4, width), BF16),
            pltpu.VMEM((2, 64), jnp.int32),
            pltpu.VMEM((2, 64), F32),
            pltpu.VMEM((NE, 16, HALF), BF16),
            pltpu.VMEM((NY, 40, HALF), BF16),
            pltpu.VMEM((80, width), BF16),
            pltpu.VMEM((80, width), BF16),
            pltpu.VMEM((2 * NX, 80, width), BF16),
            pltpu.VMEM((2 * NX, 80, width), BF16),
            pltpu.VMEM((80, width), BF16),
            pltpu.VMEM((NY - 1, 24, HALF), BF16),
            pltpu.VMEM((NY - 1, 24, HALF), BF16),
            pltpu.VMEM((NE, 8, HALF), BF16),
            pltpu.VMEM((NE - 1, 8, HALF), BF16),
            pltpu.VMEM((2, 2 * NX, 80, width), F32),
            pltpu.VMEM((2, NX, 80, width), F32),
            pltpu.VMEM((NX - 1, 2, 80, width), BF16),
            pltpu.VMEM((NX - 1, 2, 80, width), BF16),
            dma((6,)), dma((NE,)), dma((NE,)), dma((2, 7)), dma((2, 2 * NX)), dma((NY,)), dma((NY,)),
            dma((NY - 1,)), dma((NY - 1,)), dma, dma, dma((2, NX)), dma((2, NX)),
            dma((NX - 1, 2)), dma((NX - 1, 2)),
        ],
        compiler_params=pltpu.CompilerParams(
            collective_id=0, has_side_effects=True, vmem_limit_bytes=48 * 1024 * 1024
        ),
        cost_estimate=pl.CostEstimate(flops=700_000_000, bytes_accessed=2_000_000, transcendentals=51200),
        name="moe_backward",
    )(tokens, upstream, experts.T, gates.T, w_in[0].T, w_out[0])
    return out_tok, out_in.T[None], out_out[None]


def solution(mesh):
    in_specs = (
        P(("replica", "expert"), None),
        P(("replica", "expert"), None),
        P("replica", None),
        P("replica", None),
        P("expert", None, "replica"),
        P("expert", "replica", None),
    )
    out_specs = (
        P(("replica", "expert"), None),
        P("expert", None, "replica"),
        P("expert", "replica", None),
    )
    return jax.shard_map(local, mesh=mesh, in_specs=in_specs, out_specs=out_specs, check_vma=False)
```

```python
import functools

import jax
import jax.numpy as jnp
from jax import lax
from jax.experimental import pallas as pl
from jax.experimental.pallas import tpu as pltpu
from jax.sharding import PartitionSpec as P

MESH = pl.DeviceIdType.MESH
F32 = jnp.float32
BF16 = jnp.bfloat16
NZ, NH, NY, NX = 8, 2, 8, 4
NE = NZ * NH
HALF = 640


def iota(shape, dim):
    return lax.broadcasted_iota(jnp.int32, shape, dim)


def onehot(mask):
    return mask.astype(F32).astype(BF16)


def dot(a, b, dims=((1,), (0,))):
    return lax.dot_general(a, b, (dims, ((), ())), preferred_element_type=F32)


def kernel(
    tok_hbm, up_hbm, ids_hbm, gates_hbm, w1, w2,
    out_tok, out_in, out_out,
    tok, up, ids, gates,
    abuf, bbuf, X, G, W1, W2, dx, csend, crecv,
    dsend, drecv, gtwin, gfrom, gsend, grecv,
    load_sem, a_send, a_recv, w_send, w_recv, b_send, b_recv, c_send, c_recv,
    d_send, d_recv, t_send, t_recv, g_send, g_recv,
):
    e = lax.axis_index("expert")
    r = lax.axis_index("replica")
    xh, z = e // NZ, e % NZ
    y, x, core = r // (NX * 2), (r // 2) % NX, r % 2

    def to_expert(e2):
        return {"expert": e2, "replica": r}

    def to_replica(y2, x2, c2):
        return {"expert": e, "replica": (y2 * NX + x2) * 2 + c2}

    twin = to_replica(y, x, 1 - core)
    home = (y % 2) * 2 + x % 2
    column = [home, home + 1 - 2 * (home % 2), (home + 2) % 4, 3 - home]
    x_flip, y_flip = x + 1 - 2 * (x % 2), y + 1 - 2 * (y % 2)
    chip_peer = [None, to_replica(y, x_flip, core), to_replica(y_flip, x, core), to_replica(y_flip, x_flip, core)]
    def place(d):
        return (y + 2 * (d // 2)) % NY, (x + 2 * (d % 2)) % NX

    def number(d):
        y2, x2 = place(d)
        return (y2 // 2) * 2 + x2 // 2

    group_peer = [None] + [to_replica(*place(d), core) for d in range(1, NY)]
    seen = [0] + [((4 - d // 2) % 4) * 2 + d % 2 for d in range(1, NY)]
    this = number(0)
    e_peer = [None] + [to_expert((e + d) % NE) for d in range(1, NE)]
    z_peer = [None] + [to_expert(xh * NZ + (z + d) % NZ) for d in range(1, NZ)]
    mirror = to_expert((1 - xh) * NZ + z)
    far_first = (4, 3, 5, 2, 6, 1, 7)
    groups_first = (5, 3, 7, 4, 1, 2, 6)

    barrier = pltpu.get_barrier_semaphore()
    peers = [twin] + group_peer[1:] + chip_peer[1:] + e_peer[1:]
    for peer in peers:
        pl.semaphore_signal(barrier, inc=1, device_id=peer, device_id_type=MESH)

    me = home * 2 + core
    loads = [
        pltpu.make_async_copy(src, dst, load_sem.at[i])
        for i, (src, dst) in enumerate(
            (
                (tok_hbm, tok), (up_hbm, up), (ids_hbm, ids), (gates_hbm, gates),
                (w1, W1.at[me]), (w2, W2.at[me]),
            )
        )
    ]
    for load in loads:
        load.start()
    started = []

    def send(src, dst, s_sem, r_sem, peer):
        copy = pltpu.make_async_remote_copy(
            src_ref=src, dst_ref=dst, send_sem=s_sem, recv_sem=r_sem,
            device_id=peer, device_id_type=MESH,
        )
        copy.start()
        started.append(copy)

    def arrived(dst, r_sem, s_sem, peer):
        pltpu.make_async_remote_copy(
            src_ref=dst, dst_ref=dst, send_sem=s_sem, recv_sem=r_sem,
            device_id=peer, device_id_type=MESH,
        ).wait_recv()

    loads[0].wait()
    loads[1].wait()
    abuf[e] = jnp.concatenate(
        [
            tok[:, :HALF].astype(F32), tok[:, HALF:].astype(F32),
            up[:, :HALF].astype(F32), up[:, HALF:].astype(F32),
        ],
        axis=0,
    ).astype(BF16)
    pl.semaphore_wait(barrier, len(peers))

    own = abuf.at[e]
    send(own, own, a_send.at[0], a_recv.at[e], mirror)
    for d in far_first:
        send(own, own, a_send.at[d], a_recv.at[e], z_peer[d])
    loads[4].wait()
    loads[5].wait()
    weights = (W1, W2)

    def w_go(i, at, s_at, peer):
        ref = weights[i].at[at]
        send(ref, ref, w_send.at[i, s_at], w_recv.at[i, at], peer)

    def w_in(i, at, peer):
        arrived(weights[i].at[at], w_recv.at[i, at], w_send.at[i, 0], peer)

    w_go(0, me, 1, chip_peer[1])
    w_go(0, me, 2, chip_peer[2])
    w_go(0, me, 0, twin)
    w_go(1, me, 0, twin)
    w_go(1, me, 1, chip_peer[1])
    w_go(1, me, 2, chip_peer[2])

    loads[2].wait()
    loads[3].wait()
    id0, id1 = ids[0:1, :], ids[1:2, :]
    hit0, hit1 = id0 == e, id1 == e
    chosen = (hit0 | hit1).astype(F32)
    gate = jnp.where(hit0, gates[0:1, :], jnp.where(hit1, gates[1:2, :], 0.0))
    ch8 = jnp.broadcast_to(chosen, (8, 64))
    tri = onehot(iota((64, 64), 0) < iota((64, 64), 1))
    v8 = jnp.where(ch8 > 0.5, dot(ch8.astype(BF16), tri), 99.0)
    c256 = iota((64, 256), 1)
    spread = onehot(iota((64, 256), 0) == (c256 >> 4) * 4 + (c256 & 3))
    vexp = dot(v8.astype(BF16), spread)[0:1, :]
    r40 = iota((40, 256), 0)
    part = jnp.where(r40 < 32, r40 >> 3, (r40 >> 1) & 3)
    slot = jnp.where(r40 < 32, r40 & 7, 8 + (r40 & 1)).astype(F32)
    col = iota((40, 256), 1)
    pick = onehot((vexp == slot) & (part == ((col >> 2) & 3)))
    slot64 = slot[:, 0:64]
    gcol = jnp.sum(jnp.where(v8[0:1, :] == slot64, gate, 0.0), axis=1, keepdims=True)
    gcol = jnp.where(part[:, 0:1] >= 2, gcol, 1.0)

    pe = (1 - xh) * NZ + z
    arrived(abuf.at[pe], a_recv.at[pe], a_send.at[0], mirror)
    for d in far_first:
        send(abuf.at[pe], abuf.at[pe], a_send.at[NZ + d], a_recv.at[pe], z_peer[d])
    ats = [column[c] * 2 + core for c in range(4)]
    w_in(0, ats[1], chip_peer[1])
    w_go(0, ats[1], 3, chip_peer[2])
    w_go(0, ats[1], 4, twin)
    w_in(0, ats[2], chip_peer[2])
    w_go(0, ats[2], 5, twin)
    w_in(1, ats[2], chip_peer[2])
    w_go(1, ats[2], 3, chip_peer[1])
    w_go(1, ats[2], 4, twin)
    w_in(1, ats[1], chip_peer[1])
    w_go(1, ats[1], 5, twin)
    for h in range(2):
        for d in range(1, NZ):
            s = ((xh + h) % 2) * NZ + (z + d) % NZ
            arrived(abuf.at[s], a_recv.at[s], a_send.at[0], z_peer[d])
    rows = abuf[...].reshape(NE * 16, HALF)
    bbuf[this] = (dot(pick, rows) * gcol).astype(BF16)

    for d in groups_first:
        send(bbuf.at[this], bbuf.at[this], b_send.at[d], b_recv.at[this], group_peer[d])

    w_in(0, ats[3], chip_peer[2])
    w_go(0, ats[3], 6, twin)
    w_in(1, ats[3], chip_peer[1])
    w_go(1, ats[3], 6, twin)
    for d in range(1, NY):
        yy = number(d)
        arrived(bbuf.at[yy], b_recv.at[yy], b_send.at[0], group_peer[d])
    for yy in range(NY):
        for k, (out, lane) in enumerate(((X, 0), (X, HALF), (G, 0), (G, HALF))):
            out[yy * 8:yy * 8 + 8, lane:lane + HALF] = bbuf[yy, 8 * k:8 * k + 8]
    tails = jnp.concatenate([bbuf[yy, 32:40] for yy in range(NY)], axis=0)
    o64, i64 = iota((64, 64), 0), iota((64, 64), 1)
    order_tails = onehot(o64 == ((i64 >> 1) & 3) * 16 + (i64 >> 3) * 2 + (i64 & 1))
    tail = dot(order_tails, tails).astype(BF16)
    X[64:80, 0:HALF] = tail[0:16]
    X[64:80, HALF:] = tail[16:32]
    G[64:80, 0:HALF] = tail[32:48]
    G[64:80, HALF:] = tail[48:64]

    for c in range(NX):
        at = column[c] * 2 + 1 - core
        for i in range(2):
            w_in(i, at, twin)

    last = ((1,), (1,))
    hidden, width = NX * 2 * 80, 2 * HALF
    pre = dot(W1[...].reshape(hidden, width), X[...], last)
    dh = dot(W2[...].reshape(hidden, width), G[...], last)
    k0 = 0.7978845608028654
    sq = pre * pre
    t = jnp.tanh(k0 * (pre + 0.044715 * (sq * pre)))
    cdf = 0.5 * (1.0 + t)
    act = (pre * cdf).astype(BF16)
    slope = cdf + pre * (0.5 * (1.0 - t * t)) * (k0 * (1.0 + 3 * 0.044715 * sq))
    dpre32 = dh * slope
    dpre = dpre32.astype(BF16)
    dx[...] = dot(dpre32.T.astype(BF16), W1[...].reshape(hidden, width)).astype(BF16)

    q_row, q_col = iota((24, 80), 0), iota((24, 80), 1)

    def group_rows(half, yy):
        q_slot = q_row - 10 * half
        inside = (q_slot >= 0) & (q_slot < 10)
        source = jnp.where(q_slot < 8, yy * 8 + q_slot, 56 + yy * 2 + q_slot)
        return onehot(inside & (q_col == source))

    def piece(d):
        yy = number(d)
        return dot(group_rows(0, yy), dx[:, :HALF]) + dot(group_rows(1, yy), dx[:, HALF:])

    for d in groups_first:
        csend[d - 1] = piece(d).astype(BF16)
        send(csend.at[d - 1], crecv.at[d - 1], c_send.at[d - 1], c_recv.at[d - 1], group_peer[d])
    total = piece(0)

    for i, (left, right) in enumerate(((dpre, X), (act, G))):
        full = dot(left, right[...])
        for k in range(2 * NX):
            gtwin[i, k] = full[k * 80:(k + 1) * 80]
    for c in (3, 1, 2, 0):
        at = column[c] * 2 + 1 - core
        for i in range(2):
            send(gtwin.at[i, at], gfrom.at[i, column[c]], t_send.at[i, c], t_recv.at[i, column[c]], twin)

    def both_cores(c, i):
        arrived(gfrom.at[i, column[c]], t_recv.at[i, column[c]], t_send.at[i, c], twin)
        return gtwin[i, column[c] * 2 + core] + gfrom[i, column[c]]

    def g_go(c, i, value, peer):
        gsend[c - 1, i] = value.astype(BF16)
        send(gsend.at[c - 1, i], grecv.at[c - 1, i], g_send.at[c - 1, i], g_recv.at[c - 1, i], peer)

    def g_in(c, i, peer):
        arrived(grecv.at[c - 1, i], g_recv.at[c - 1, i], g_send.at[c - 1, i], peer)
        return grecv[c - 1, i].astype(F32)

    g_go(3, 0, both_cores(3, 0), chip_peer[2])
    g_go(3, 1, both_cores(3, 1), chip_peer[2])

    r64 = iota((128, 64), 0)
    gather = onehot(iota((128, 64), 1) == (r64 >> 3) * 4 + (r64 & 3))
    v_row = dot(gather, v8.astype(BF16), last)[:, 0:1]
    t_row, t_col = iota((128, 24), 0), iota((128, 24), 1)
    t_half = (t_col >= 10).astype(jnp.int32)
    t_slot = jnp.where(t_col < 20, t_col - 10 * t_half, 50).astype(F32)
    back = onehot((v_row == t_slot) & (((t_row >> 2) & 1) == t_half))

    for d in range(1, NY):
        arrived(crecv.at[d - 1], c_recv.at[d - 1], c_send.at[d - 1], group_peer[seen[d]])
        total = total + crecv[d - 1].astype(F32)
    spread_rows = dot(back, total.astype(BF16))
    dsend[...] = spread_rows.reshape(NE, 8, HALF).astype(BF16)
    for d in (8, 12, 4, 9, 7, 10, 6, 11, 5, 13, 3, 14, 2, 15, 1):
        pltpu.make_async_remote_copy(
            src_ref=dsend.at[(e + d) % NE], dst_ref=drecv.at[d - 1],
            send_sem=d_send, recv_sem=d_recv, device_id=e_peer[d], device_id_type=MESH,
        ).start()

    for i in range(2):
        g_go(1, i, both_cores(1, i) + g_in(3, i, chip_peer[2]), chip_peer[1])
        g_go(2, i, both_cores(2, i), chip_peer[2])
    landed = pltpu.make_async_remote_copy(
        src_ref=drecv, dst_ref=drecv, send_sem=d_send, recv_sem=d_recv,
        device_id=e_peer[1], device_id_type=MESH,
    )
    landed.wait_recv()
    res = dsend[e].astype(F32)
    for d in range(1, NE):
        res = res + drecv[d - 1].astype(F32)
    out_tok[:, :HALF] = res[0:4].astype(BF16)
    out_tok[:, HALF:] = res[4:8].astype(BF16)
    for i, out in ((0, out_in), (1, out_out)):
        out[...] = both_cores(0, i) + g_in(1, i, chip_peer[1]) + g_in(2, i, chip_peer[2])
    landed.wait_send()
    for copy in started:
        copy.wait_send()


def local(tokens, upstream, experts, gates, w_in, w_out):
    vmem = pl.BlockSpec(memory_space=pltpu.VMEM)
    dma = pltpu.SemaphoreType.DMA
    width = 2 * HALF
    out_tok, out_in, out_out = pl.pallas_call(
        kernel,
        out_shape=(
            jax.ShapeDtypeStruct((4, width), BF16),
            jax.ShapeDtypeStruct((80, width), F32),
            jax.ShapeDtypeStruct((80, width), F32),
        ),
        in_specs=[pl.BlockSpec(memory_space=pltpu.HBM)] * 6,
        out_specs=(vmem, vmem, vmem),
        scratch_shapes=[
            pltpu.VMEM((4, width), BF16),
            pltpu.VMEM((4, width), BF16),
            pltpu.VMEM((2, 64), jnp.int32),
            pltpu.VMEM((2, 64), F32),
            pltpu.VMEM((NE, 16, HALF), BF16),
            pltpu.VMEM((NY, 40, HALF), BF16),
            pltpu.VMEM((80, width), BF16),
            pltpu.VMEM((80, width), BF16),
            pltpu.VMEM((2 * NX, 80, width), BF16),
            pltpu.VMEM((2 * NX, 80, width), BF16),
            pltpu.VMEM((80, width), BF16),
            pltpu.VMEM((NY - 1, 24, HALF), BF16),
            pltpu.VMEM((NY - 1, 24, HALF), BF16),
            pltpu.VMEM((NE, 8, HALF), BF16),
            pltpu.VMEM((NE - 1, 8, HALF), BF16),
            pltpu.VMEM((2, 2 * NX, 80, width), F32),
            pltpu.VMEM((2, NX, 80, width), F32),
            pltpu.VMEM((NX - 1, 2, 80, width), BF16),
            pltpu.VMEM((NX - 1, 2, 80, width), BF16),
            dma((6,)), dma((NE,)), dma((NE,)), dma((2, 7)), dma((2, 2 * NX)), dma((NY,)), dma((NY,)),
            dma((NY - 1,)), dma((NY - 1,)), dma, dma, dma((2, NX)), dma((2, NX)),
            dma((NX - 1, 2)), dma((NX - 1, 2)),
        ],
        compiler_params=pltpu.CompilerParams(
            collective_id=0, has_side_effects=True, vmem_limit_bytes=62 * 1024 * 1024
        ),
        cost_estimate=pl.CostEstimate(flops=700_000_000, bytes_accessed=2_000_000, transcendentals=51200),
        name="moe_backward",
    )(tokens, upstream, experts.T, gates.T, w_in[0].T, w_out[0])
    return out_tok, out_in.T[None], out_out[None]


def solution(mesh):
    in_specs = (
        P(("replica", "expert"), None),
        P(("replica", "expert"), None),
        P("replica", None),
        P("replica", None),
        P("expert", None, "replica"),
        P("expert", "replica", None),
    )
    out_specs = (
        P(("replica", "expert"), None),
        P("expert", None, "replica"),
        P("expert", "replica", None),
    )
    return jax.shard_map(local, mesh=mesh, in_specs=in_specs, out_specs=out_specs, check_vma=False)
```

```python
import functools

import jax
import jax.numpy as jnp
from jax import lax
from jax.experimental import pallas as pl
from jax.experimental.pallas import tpu as pltpu
from jax.sharding import PartitionSpec as P

MESH = pl.DeviceIdType.MESH
F32 = jnp.float32
BF16 = jnp.bfloat16
NZ, NH, NY, NX = 8, 2, 8, 4
NE = NZ * NH
HALF = 640


def iota(shape, dim):
    return lax.broadcasted_iota(jnp.int32, shape, dim)


def onehot(mask):
    return mask.astype(F32).astype(BF16)


def dot(a, b, dims=((1,), (0,))):
    return lax.dot_general(a, b, (dims, ((), ())), preferred_element_type=F32)


def kernel(
    tok_hbm, up_hbm, ids_hbm, gates_hbm, w1, w2,
    out_tok, out_in, out_out,
    tok, up, ids, gates,
    abuf, bbuf, X, G, W1, W2, dx, csend, crecv,
    dsend, drecv, gtwin, gfrom, gsend, grecv,
    load_sem, a_send, a_recv, w_send, w_recv, b_send, b_recv, c_send, c_recv,
    d_send, d_recv, t_send, t_recv, g_send, g_recv,
):
    e = lax.axis_index("expert")
    r = lax.axis_index("replica")
    xh, z = e // NZ, e % NZ
    y, x, core = r // (NX * 2), (r // 2) % NX, r % 2

    def to_expert(e2):
        return {"expert": e2, "replica": r}

    def to_replica(y2, x2, c2):
        return {"expert": e, "replica": (y2 * NX + x2) * 2 + c2}

    twin = to_replica(y, x, 1 - core)
    home = (y % 2) * 2 + x % 2
    column = [home, home + 1 - 2 * (home % 2), (home + 2) % 4, 3 - home]
    x_flip, y_flip = x + 1 - 2 * (x % 2), y + 1 - 2 * (y % 2)
    chip_peer = [None, to_replica(y, x_flip, core), to_replica(y_flip, x, core), to_replica(y_flip, x_flip, core)]
    def place(d):
        return (y + 2 * (d // 2)) % NY, (x + 2 * (d % 2)) % NX

    def number(d):
        y2, x2 = place(d)
        return (y2 // 2) * 2 + x2 // 2

    group_peer = [None] + [to_replica(*place(d), core) for d in range(1, NY)]
    seen = [0] + [((4 - d // 2) % 4) * 2 + d % 2 for d in range(1, NY)]
    this = number(0)
    e_peer = [None] + [to_expert((e + d) % NE) for d in range(1, NE)]
    z_peer = [None] + [to_expert(xh * NZ + (z + d) % NZ) for d in range(1, NZ)]
    mirror = to_expert((1 - xh) * NZ + z)
    far_first = (4, 3, 5, 2, 6, 1, 7)
    groups_first = (5, 3, 7, 4, 1, 2, 6)

    barrier = pltpu.get_barrier_semaphore()
    peers = [twin] + group_peer[1:] + chip_peer[1:] + e_peer[1:]
    for peer in peers:
        pl.semaphore_signal(barrier, inc=1, device_id=peer, device_id_type=MESH)

    me = home * 2 + core
    loads = [
        pltpu.make_async_copy(src, dst, load_sem.at[i])
        for i, (src, dst) in enumerate(
            (
                (tok_hbm, tok), (up_hbm, up), (ids_hbm, ids), (gates_hbm, gates),
                (w1, W1.at[me]), (w2, W2.at[me]),
            )
        )
    ]
    for load in loads:
        load.start()
    started = []

    def send(src, dst, s_sem, r_sem, peer):
        copy = pltpu.make_async_remote_copy(
            src_ref=src, dst_ref=dst, send_sem=s_sem, recv_sem=r_sem,
            device_id=peer, device_id_type=MESH,
        )
        copy.start()
        started.append(copy)

    def arrived(dst, r_sem, s_sem, peer):
        pltpu.make_async_remote_copy(
            src_ref=dst, dst_ref=dst, send_sem=s_sem, recv_sem=r_sem,
            device_id=peer, device_id_type=MESH,
        ).wait_recv()

    loads[0].wait()
    loads[1].wait()
    abuf[e] = jnp.concatenate(
        [
            tok[:, :HALF].astype(F32), tok[:, HALF:].astype(F32),
            up[:, :HALF].astype(F32), up[:, HALF:].astype(F32),
        ],
        axis=0,
    ).astype(BF16)
    pl.semaphore_wait(barrier, len(peers))

    own = abuf.at[e]
    send(own, own, a_send.at[0], a_recv.at[e], mirror)
    for d in far_first:
        send(own, own, a_send.at[d], a_recv.at[e], z_peer[d])
    loads[4].wait()
    loads[5].wait()
    weights = (W1, W2)

    def w_go(i, at, s_at, peer):
        ref = weights[i].at[at]
        send(ref, ref, w_send.at[i, s_at], w_recv.at[i, at], peer)

    def w_in(i, at, peer):
        arrived(weights[i].at[at], w_recv.at[i, at], w_send.at[i, 0], peer)

    w_go(0, me, 1, chip_peer[1])
    w_go(0, me, 2, chip_peer[2])
    w_go(0, me, 0, twin)
    w_go(1, me, 0, twin)
    w_go(1, me, 1, chip_peer[1])
    w_go(1, me, 2, chip_peer[2])

    loads[2].wait()
    loads[3].wait()
    id0, id1 = ids[0:1, :], ids[1:2, :]
    hit0, hit1 = id0 == e, id1 == e
    chosen = (hit0 | hit1).astype(F32)
    gate = jnp.where(hit0, gates[0:1, :], jnp.where(hit1, gates[1:2, :], 0.0))
    ch8 = jnp.broadcast_to(chosen, (8, 64))
    tri = onehot(iota((64, 64), 0) < iota((64, 64), 1))
    v8 = jnp.where(ch8 > 0.5, dot(ch8.astype(BF16), tri), 99.0)
    c256 = iota((64, 256), 1)
    spread = onehot(iota((64, 256), 0) == (c256 >> 4) * 4 + (c256 & 3))
    vexp = dot(v8.astype(BF16), spread)[0:1, :]
    r40 = iota((40, 256), 0)
    part = jnp.where(r40 < 32, r40 >> 3, (r40 >> 1) & 3)
    slot = jnp.where(r40 < 32, r40 & 7, 8 + (r40 & 1)).astype(F32)
    col = iota((40, 256), 1)
    pick = onehot((vexp == slot) & (part == ((col >> 2) & 3)))
    slot64 = slot[:, 0:64]
    gcol = jnp.sum(jnp.where(v8[0:1, :] == slot64, gate, 0.0), axis=1, keepdims=True)
    gcol = jnp.where(part[:, 0:1] >= 2, gcol, 1.0)

    pe = (1 - xh) * NZ + z
    arrived(abuf.at[pe], a_recv.at[pe], a_send.at[0], mirror)
    for d in far_first:
        send(abuf.at[pe], abuf.at[pe], a_send.at[NZ + d], a_recv.at[pe], z_peer[d])
    ats = [column[c] * 2 + core for c in range(4)]
    w_in(0, ats[1], chip_peer[1])
    w_go(0, ats[1], 3, chip_peer[2])
    w_go(0, ats[1], 4, twin)
    w_in(0, ats[2], chip_peer[2])
    w_go(0, ats[2], 5, twin)
    w_in(1, ats[2], chip_peer[2])
    w_go(1, ats[2], 3, chip_peer[1])
    w_go(1, ats[2], 4, twin)
    w_in(1, ats[1], chip_peer[1])
    w_go(1, ats[1], 5, twin)
    for h in range(2):
        for d in range(1, NZ):
            s = ((xh + h) % 2) * NZ + (z + d) % NZ
            arrived(abuf.at[s], a_recv.at[s], a_send.at[0], z_peer[d])
    rows = abuf[...].reshape(NE * 16, HALF)
    bbuf[this] = (dot(pick, rows) * gcol).astype(BF16)

    for d in groups_first:
        send(bbuf.at[this], bbuf.at[this], b_send.at[d], b_recv.at[this], group_peer[d])

    w_in(0, ats[3], chip_peer[2])
    w_go(0, ats[3], 6, twin)
    w_in(1, ats[3], chip_peer[1])
    w_go(1, ats[3], 6, twin)
    for d in range(1, NY):
        yy = number(d)
        arrived(bbuf.at[yy], b_recv.at[yy], b_send.at[0], group_peer[d])
    for yy in range(NY):
        for k, (out, lane) in enumerate(((X, 0), (X, HALF), (G, 0), (G, HALF))):
            out[yy * 8:yy * 8 + 8, lane:lane + HALF] = bbuf[yy, 8 * k:8 * k + 8]
    tails = jnp.concatenate([bbuf[yy, 32:40] for yy in range(NY)], axis=0)
    o64, i64 = iota((64, 64), 0), iota((64, 64), 1)
    order_tails = onehot(o64 == ((i64 >> 1) & 3) * 16 + (i64 >> 3) * 2 + (i64 & 1))
    tail = dot(order_tails, tails).astype(BF16)
    X[64:80, 0:HALF] = tail[0:16]
    X[64:80, HALF:] = tail[16:32]
    G[64:80, 0:HALF] = tail[32:48]
    G[64:80, HALF:] = tail[48:64]

    for c in range(NX):
        at = column[c] * 2 + 1 - core
        for i in range(2):
            w_in(i, at, twin)

    last = ((1,), (1,))
    hidden, width = NX * 2 * 80, 2 * HALF
    pre = dot(W1[...].reshape(hidden, width), X[...], last)
    dh = dot(W2[...].reshape(hidden, width), G[...], last)
    k0 = 0.7978845608028654
    sq = pre * pre
    t = jnp.tanh(k0 * (pre + 0.044715 * (sq * pre)))
    cdf = 0.5 * (1.0 + t)
    act = (pre * cdf).astype(BF16)
    slope = cdf + pre * (0.5 * (1.0 - t * t)) * (k0 * (1.0 + 3 * 0.044715 * sq))
    dpre32 = dh * slope
    dpre = dpre32.astype(BF16)
    dx[...] = dot(dpre32.T.astype(BF16), W1[...].reshape(hidden, width)).astype(BF16)

    q_row, q_col = iota((24, 80), 0), iota((24, 80), 1)

    def group_rows(half, yy):
        q_slot = q_row - 10 * half
        inside = (q_slot >= 0) & (q_slot < 10)
        source = jnp.where(q_slot < 8, yy * 8 + q_slot, 56 + yy * 2 + q_slot)
        return onehot(inside & (q_col == source))

    def piece(d):
        yy = number(d)
        return dot(group_rows(0, yy), dx[:, :HALF]) + dot(group_rows(1, yy), dx[:, HALF:])

    for d in groups_first:
        csend[d - 1] = piece(d).astype(BF16)
        send(csend.at[d - 1], crecv.at[d - 1], c_send.at[d - 1], c_recv.at[d - 1], group_peer[d])
    total = piece(0)

    for i, (left, right) in enumerate(((dpre, X), (act, G))):
        full = dot(left, right[...])
        for k in range(2 * NX):
            gtwin[i, k] = full[k * 80:(k + 1) * 80]
        for c in (3, 2, 1, 0):
            at = column[c] * 2 + 1 - core
            send(gtwin.at[i, at], gfrom.at[i, column[c]], t_send.at[i, c], t_recv.at[i, column[c]], twin)

    def both_cores(c, i):
        arrived(gfrom.at[i, column[c]], t_recv.at[i, column[c]], t_send.at[i, c], twin)
        return gtwin[i, column[c] * 2 + core] + gfrom[i, column[c]]

    def g_go(c, i, value, peer):
        gsend[c - 1, i] = value.astype(BF16)
        send(gsend.at[c - 1, i], grecv.at[c - 1, i], g_send.at[c - 1, i], g_recv.at[c - 1, i], peer)

    def g_in(c, i, peer):
        arrived(grecv.at[c - 1, i], g_recv.at[c - 1, i], g_send.at[c - 1, i], peer)
        return grecv[c - 1, i].astype(F32)

    g_go(3, 0, both_cores(3, 0), chip_peer[2])
    g_go(3, 1, both_cores(3, 1), chip_peer[2])
    g_go(2, 0, both_cores(2, 0), chip_peer[2])
    g_go(2, 1, both_cores(2, 1), chip_peer[2])

    r64 = iota((128, 64), 0)
    gather = onehot(iota((128, 64), 1) == (r64 >> 3) * 4 + (r64 & 3))
    v_row = dot(gather, v8.astype(BF16), last)[:, 0:1]
    t_row, t_col = iota((128, 24), 0), iota((128, 24), 1)
    t_half = (t_col >= 10).astype(jnp.int32)
    t_slot = jnp.where(t_col < 20, t_col - 10 * t_half, 50).astype(F32)
    back = onehot((v_row == t_slot) & (((t_row >> 2) & 1) == t_half))

    for d in range(1, NY):
        arrived(crecv.at[d - 1], c_recv.at[d - 1], c_send.at[d - 1], group_peer[seen[d]])
        total = total + crecv[d - 1].astype(F32)
    spread_rows = dot(back, total.astype(BF16))
    dsend[...] = spread_rows.reshape(NE, 8, HALF).astype(BF16)
    for d in (8, 12, 4, 9, 7, 10, 6, 11, 5, 13, 3, 14, 2, 15, 1):
        pltpu.make_async_remote_copy(
            src_ref=dsend.at[(e + d) % NE], dst_ref=drecv.at[d - 1],
            send_sem=d_send, recv_sem=d_recv, device_id=e_peer[d], device_id_type=MESH,
        ).start()

    for i in range(2):
        g_go(1, i, both_cores(1, i) + g_in(3, i, chip_peer[2]), chip_peer[1])
    landed = pltpu.make_async_remote_copy(
        src_ref=drecv, dst_ref=drecv, send_sem=d_send, recv_sem=d_recv,
        device_id=e_peer[1], device_id_type=MESH,
    )
    landed.wait_recv()
    res = dsend[e].astype(F32)
    for d in range(1, NE):
        res = res + drecv[d - 1].astype(F32)
    out_tok[:, :HALF] = res[0:4].astype(BF16)
    out_tok[:, HALF:] = res[4:8].astype(BF16)
    for i, out in ((0, out_in), (1, out_out)):
        out[...] = both_cores(0, i) + g_in(1, i, chip_peer[1]) + g_in(2, i, chip_peer[2])
    landed.wait_send()
    for copy in started:
        copy.wait_send()


def local(tokens, upstream, experts, gates, w_in, w_out):
    vmem = pl.BlockSpec(memory_space=pltpu.VMEM)

    def hbm(a):
        return pltpu.with_memory_space_constraint(a, pltpu.HBM)

    dma = pltpu.SemaphoreType.DMA
    width = 2 * HALF
    out_tok, out_in, out_out = pl.pallas_call(
        kernel,
        out_shape=(
            pltpu.VMEM((4, width), BF16),
            pltpu.VMEM((80, width), F32),
            pltpu.VMEM((80, width), F32),
        ),
        in_specs=[pl.BlockSpec(memory_space=pltpu.HBM)] * 6,
        out_specs=(vmem, vmem, vmem),
        scratch_shapes=[
            pltpu.VMEM((4, width), BF16),
            pltpu.VMEM((4, width), BF16),
            pltpu.VMEM((2, 64), jnp.int32),
            pltpu.VMEM((2, 64), F32),
            pltpu.VMEM((NE, 16, HALF), BF16),
            pltpu.VMEM((NY, 40, HALF), BF16),
            pltpu.VMEM((80, width), BF16),
            pltpu.VMEM((80, width), BF16),
            pltpu.VMEM((2 * NX, 80, width), BF16),
            pltpu.VMEM((2 * NX, 80, width), BF16),
            pltpu.VMEM((80, width), BF16),
            pltpu.VMEM((NY - 1, 24, HALF), BF16),
            pltpu.VMEM((NY - 1, 24, HALF), BF16),
            pltpu.VMEM((NE, 8, HALF), BF16),
            pltpu.VMEM((NE - 1, 8, HALF), BF16),
            pltpu.VMEM((2, 2 * NX, 80, width), F32),
            pltpu.VMEM((2, NX, 80, width), F32),
            pltpu.VMEM((NX - 1, 2, 80, width), BF16),
            pltpu.VMEM((NX - 1, 2, 80, width), BF16),
            dma((6,)), dma((NE,)), dma((NE,)), dma((2, 7)), dma((2, 2 * NX)), dma((NY,)), dma((NY,)),
            dma((NY - 1,)), dma((NY - 1,)), dma, dma, dma((2, NX)), dma((2, NX)),
            dma((NX - 1, 2)), dma((NX - 1, 2)),
        ],
        compiler_params=pltpu.CompilerParams(
            collective_id=0, has_side_effects=True, vmem_limit_bytes=56 * 1024 * 1024
        ),
        cost_estimate=pl.CostEstimate(flops=700_000_000, bytes_accessed=2_000_000, transcendentals=51200),
        name="moe_backward",
    )(*(hbm(a) for a in (tokens, upstream, experts.T, gates.T, w_in[0].T, w_out[0])))
    return out_tok, out_in.T[None], out_out[None]


def solution(mesh):
    in_specs = (
        P(("replica", "expert"), None),
        P(("replica", "expert"), None),
        P("replica", None),
        P("replica", None),
        P("expert", None, "replica"),
        P("expert", "replica", None),
    )
    out_specs = (
        P(("replica", "expert"), None),
        P("expert", None, "replica"),
        P("expert", "replica", None),
    )
    return jax.shard_map(local, mesh=mesh, in_specs=in_specs, out_specs=out_specs, check_vma=False)
```

```python
import functools

import jax
import jax.numpy as jnp
from jax import lax
from jax.experimental import pallas as pl
from jax.experimental.pallas import tpu as pltpu
from jax.sharding import PartitionSpec as P

MESH = pl.DeviceIdType.MESH
F32 = jnp.float32
BF16 = jnp.bfloat16
NZ, NH, NY, NX = 8, 2, 8, 4
NE = NZ * NH
HALF = 640


def iota(shape, dim):
    return lax.broadcasted_iota(jnp.int32, shape, dim)


def onehot(mask):
    return mask.astype(F32).astype(BF16)


def dot(a, b, dims=((1,), (0,))):
    return lax.dot_general(a, b, (dims, ((), ())), preferred_element_type=F32)


def kernel(
    tok_hbm, up_hbm, ids_hbm, gates_hbm, w1, w2,
    out_tok, out_in, out_out,
    tok, up, ids, gates,
    abuf, bbuf, X, G, W1, W2, dx, csend, crecv,
    dsend, drecv, gtwin, gfrom, gsend, grecv,
    load_sem, a_send, a_recv, w_send, w_recv, b_send, b_recv, c_send, c_recv,
    d_send, d_recv, t_send, t_recv, g_send, g_recv,
):
    e = lax.axis_index("expert")
    r = lax.axis_index("replica")
    xh, z = e // NZ, e % NZ
    y, x, core = r // (NX * 2), (r // 2) % NX, r % 2

    def to_expert(e2):
        return {"expert": e2, "replica": r}

    def to_replica(y2, x2, c2):
        return {"expert": e, "replica": (y2 * NX + x2) * 2 + c2}

    twin = to_replica(y, x, 1 - core)
    home = (y % 2) * 2 + x % 2
    column = [home, home + 1 - 2 * (home % 2), (home + 2) % 4, 3 - home]
    x_flip, y_flip = x + 1 - 2 * (x % 2), y + 1 - 2 * (y % 2)
    chip_peer = [None, to_replica(y, x_flip, core), to_replica(y_flip, x, core), to_replica(y_flip, x_flip, core)]
    def place(d):
        return (y + 2 * (d // 2)) % NY, (x + 2 * (d % 2)) % NX

    def number(d):
        y2, x2 = place(d)
        return (y2 // 2) * 2 + x2 // 2

    group_peer = [None] + [to_replica(*place(d), core) for d in range(1, NY)]
    seen = [0] + [((4 - d // 2) % 4) * 2 + d % 2 for d in range(1, NY)]
    this = number(0)
    e_peer = [None] + [to_expert((e + d) % NE) for d in range(1, NE)]
    z_peer = [None] + [to_expert(xh * NZ + (z + d) % NZ) for d in range(1, NZ)]
    mirror = to_expert((1 - xh) * NZ + z)
    far_first = (4, 3, 5, 2, 6, 1, 7)
    groups_first = (5, 3, 7, 4, 1, 2, 6)

    barrier = pltpu.get_barrier_semaphore()
    peers = [twin] + group_peer[1:] + chip_peer[1:] + e_peer[1:]
    for peer in peers:
        pl.semaphore_signal(barrier, inc=1, device_id=peer, device_id_type=MESH)

    me = home * 2 + core
    loads = [
        pltpu.make_async_copy(src, dst, load_sem.at[i])
        for i, (src, dst) in enumerate(
            (
                (tok_hbm, tok), (up_hbm, up), (ids_hbm, ids), (gates_hbm, gates),
                (w1, W1.at[me]), (w2, W2.at[me]),
            )
        )
    ]
    for load in loads:
        load.start()
    started = []

    def send(src, dst, s_sem, r_sem, peer):
        copy = pltpu.make_async_remote_copy(
            src_ref=src, dst_ref=dst, send_sem=s_sem, recv_sem=r_sem,
            device_id=peer, device_id_type=MESH,
        )
        copy.start()
        started.append(copy)

    def arrived(dst, r_sem, s_sem, peer):
        pltpu.make_async_remote_copy(
            src_ref=dst, dst_ref=dst, send_sem=s_sem, recv_sem=r_sem,
            device_id=peer, device_id_type=MESH,
        ).wait_recv()

    loads[0].wait()
    loads[1].wait()
    abuf[e] = jnp.concatenate(
        [
            tok[:, :HALF].astype(F32), tok[:, HALF:].astype(F32),
            up[:, :HALF].astype(F32), up[:, HALF:].astype(F32),
        ],
        axis=0,
    ).astype(BF16)
    pl.semaphore_wait(barrier, len(peers))

    own = abuf.at[e]
    send(own, own, a_send.at[0], a_recv.at[e], mirror)
    for d in far_first:
        send(own, own, a_send.at[d], a_recv.at[e], z_peer[d])
    loads[4].wait()
    loads[5].wait()
    weights = (W1, W2)

    def w_go(i, at, s_at, peer):
        ref = weights[i].at[at]
        send(ref, ref, w_send.at[i, s_at], w_recv.at[i, at], peer)

    def w_in(i, at, peer):
        arrived(weights[i].at[at], w_recv.at[i, at], w_send.at[i, 0], peer)

    w_go(0, me, 1, chip_peer[1])
    w_go(0, me, 2, chip_peer[2])
    w_go(0, me, 0, twin)
    w_go(1, me, 0, twin)
    w_go(1, me, 1, chip_peer[1])
    w_go(1, me, 2, chip_peer[2])

    loads[2].wait()
    loads[3].wait()
    id0, id1 = ids[0:1, :], ids[1:2, :]
    hit0, hit1 = id0 == e, id1 == e
    chosen = (hit0 | hit1).astype(F32)
    gate = jnp.where(hit0, gates[0:1, :], jnp.where(hit1, gates[1:2, :], 0.0))
    ch8 = jnp.broadcast_to(chosen, (8, 64))
    tri = onehot(iota((64, 64), 0) < iota((64, 64), 1))
    v8 = jnp.where(ch8 > 0.5, dot(ch8.astype(BF16), tri), 99.0)
    c256 = iota((64, 256), 1)
    spread = onehot(iota((64, 256), 0) == (c256 >> 4) * 4 + (c256 & 3))
    vexp = dot(v8.astype(BF16), spread)[0:1, :]
    r40 = iota((40, 256), 0)
    part = jnp.where(r40 < 32, r40 >> 3, (r40 >> 1) & 3)
    slot = jnp.where(r40 < 32, r40 & 7, 8 + (r40 & 1)).astype(F32)
    col = iota((40, 256), 1)
    pick = onehot((vexp == slot) & (part == ((col >> 2) & 3)))
    slot64 = slot[:, 0:64]
    gcol = jnp.sum(jnp.where(v8[0:1, :] == slot64, gate, 0.0), axis=1, keepdims=True)
    gcol = jnp.where(part[:, 0:1] >= 2, gcol, 1.0)

    pe = (1 - xh) * NZ + z
    arrived(abuf.at[pe], a_recv.at[pe], a_send.at[0], mirror)
    for d in far_first:
        send(abuf.at[pe], abuf.at[pe], a_send.at[NZ + d], a_recv.at[pe], z_peer[d])
    ats = [column[c] * 2 + core for c in range(4)]
    w_in(0, ats[1], chip_peer[1])
    w_go(0, ats[1], 3, chip_peer[2])
    w_go(0, ats[1], 4, twin)
    w_in(0, ats[2], chip_peer[2])
    w_go(0, ats[2], 5, twin)
    w_in(1, ats[2], chip_peer[2])
    w_go(1, ats[2], 3, chip_peer[1])
    w_go(1, ats[2], 4, twin)
    w_in(1, ats[1], chip_peer[1])
    w_go(1, ats[1], 5, twin)
    for h in range(2):
        for d in range(1, NZ):
            s = ((xh + h) % 2) * NZ + (z + d) % NZ
            arrived(abuf.at[s], a_recv.at[s], a_send.at[0], z_peer[d])
    rows = abuf[...].reshape(NE * 16, HALF)
    bbuf[this] = (dot(pick, rows) * gcol).astype(BF16)

    for d in groups_first:
        send(bbuf.at[this], bbuf.at[this], b_send.at[d], b_recv.at[this], group_peer[d])

    w_in(0, ats[3], chip_peer[2])
    w_go(0, ats[3], 6, twin)
    w_in(1, ats[3], chip_peer[1])
    w_go(1, ats[3], 6, twin)
    for d in range(1, NY):
        yy = number(d)
        arrived(bbuf.at[yy], b_recv.at[yy], b_send.at[0], group_peer[d])
    for yy in range(NY):
        for k, (out, lane) in enumerate(((X, 0), (X, HALF), (G, 0), (G, HALF))):
            out[yy * 8:yy * 8 + 8, lane:lane + HALF] = bbuf[yy, 8 * k:8 * k + 8]
    tails = jnp.concatenate([bbuf[yy, 32:40] for yy in range(NY)], axis=0)
    o64, i64 = iota((64, 64), 0), iota((64, 64), 1)
    order_tails = onehot(o64 == ((i64 >> 1) & 3) * 16 + (i64 >> 3) * 2 + (i64 & 1))
    tail = dot(order_tails, tails).astype(BF16)
    X[64:80, 0:HALF] = tail[0:16]
    X[64:80, HALF:] = tail[16:32]
    G[64:80, 0:HALF] = tail[32:48]
    G[64:80, HALF:] = tail[48:64]

    for c in range(NX):
        at = column[c] * 2 + 1 - core
        for i in range(2):
            w_in(i, at, twin)

    last = ((1,), (1,))
    hidden, width = NX * 2 * 80, 2 * HALF
    pre = dot(W1[...].reshape(hidden, width), X[...], last)
    dh = dot(W2[...].reshape(hidden, width), G[...], last)
    k0 = 0.7978845608028654
    sq = pre * pre
    t = jnp.tanh(k0 * (pre + 0.044715 * (sq * pre)))
    cdf = 0.5 * (1.0 + t)
    act = (pre * cdf).astype(BF16)
    slope = cdf + pre * (0.5 * (1.0 - t * t)) * (k0 * (1.0 + 3 * 0.044715 * sq))
    dpre32 = dh * slope
    dpre = dpre32.astype(BF16)
    dx[...] = dot(dpre32.T.astype(BF16), W1[...].reshape(hidden, width)).astype(BF16)

    q_row, q_col = iota((24, 80), 0), iota((24, 80), 1)

    def group_rows(half, yy):
        q_slot = q_row - 10 * half
        inside = (q_slot >= 0) & (q_slot < 10)
        source = jnp.where(q_slot < 8, yy * 8 + q_slot, 56 + yy * 2 + q_slot)
        return onehot(inside & (q_col == source))

    def piece(d):
        yy = number(d)
        return dot(group_rows(0, yy), dx[:, :HALF]) + dot(group_rows(1, yy), dx[:, HALF:])

    for d in groups_first:
        csend[d - 1] = piece(d).astype(BF16)
        send(csend.at[d - 1], crecv.at[d - 1], c_send.at[d - 1], c_recv.at[d - 1], group_peer[d])
    total = piece(0)

    def to_twin(c, i):
        at = column[c] * 2 + 1 - core
        send(gtwin.at[i, at], gfrom.at[i, column[c]], t_send.at[i, c], t_recv.at[i, column[c]], twin)

    for i, (left, right) in enumerate(((dpre, X), (act, G))):
        full = dot(left, right[...])
        for k in range(2 * NX):
            gtwin[i, k] = full[k * 80:(k + 1) * 80].astype(BF16)
        to_twin(3, i)
    to_twin(2, 0)
    to_twin(2, 1)

    def both_cores(c, i):
        arrived(gfrom.at[i, column[c]], t_recv.at[i, column[c]], t_send.at[i, c], twin)
        return gtwin[i, column[c] * 2 + core].astype(F32) + gfrom[i, column[c]].astype(F32)

    def g_go(c, i, value, peer):
        gsend[c - 1, i] = value.astype(BF16)
        send(gsend.at[c - 1, i], grecv.at[c - 1, i], g_send.at[c - 1, i], g_recv.at[c - 1, i], peer)

    def g_in(c, i, peer):
        arrived(grecv.at[c - 1, i], g_recv.at[c - 1, i], g_send.at[c - 1, i], peer)
        return grecv[c - 1, i].astype(F32)

    g_go(3, 0, both_cores(3, 0), chip_peer[2])
    g_go(3, 1, both_cores(3, 1), chip_peer[2])
    for c in (1, 0):
        for i in range(2):
            to_twin(c, i)
    g_go(2, 0, both_cores(2, 0), chip_peer[2])
    g_go(2, 1, both_cores(2, 1), chip_peer[2])

    r64 = iota((128, 64), 0)
    gather = onehot(iota((128, 64), 1) == (r64 >> 3) * 4 + (r64 & 3))
    v_row = dot(gather, v8.astype(BF16), last)[:, 0:1]
    t_row, t_col = iota((128, 24), 0), iota((128, 24), 1)
    t_half = (t_col >= 10).astype(jnp.int32)
    t_slot = jnp.where(t_col < 20, t_col - 10 * t_half, 50).astype(F32)
    back = onehot((v_row == t_slot) & (((t_row >> 2) & 1) == t_half))

    for d in range(1, NY):
        arrived(crecv.at[d - 1], c_recv.at[d - 1], c_send.at[d - 1], group_peer[seen[d]])
        total = total + crecv[d - 1].astype(F32)
    spread_rows = dot(back, total.astype(BF16))
    dsend[...] = spread_rows.reshape(NE, 8, HALF).astype(BF16)
    for d in (8, 12, 4, 9, 7, 10, 6, 11, 5, 13, 3, 14, 2, 15, 1):
        pltpu.make_async_remote_copy(
            src_ref=dsend.at[(e + d) % NE], dst_ref=drecv.at[d - 1],
            send_sem=d_send, recv_sem=d_recv, device_id=e_peer[d], device_id_type=MESH,
        ).start()

    for i in range(2):
        g_go(1, i, both_cores(1, i) + g_in(3, i, chip_peer[2]), chip_peer[1])
    landed = pltpu.make_async_remote_copy(
        src_ref=drecv, dst_ref=drecv, send_sem=d_send, recv_sem=d_recv,
        device_id=e_peer[1], device_id_type=MESH,
    )
    landed.wait_recv()
    res = dsend[e].astype(F32)
    for d in range(1, NE):
        res = res + drecv[d - 1].astype(F32)
    out_tok[:, :HALF] = res[0:4].astype(BF16)
    out_tok[:, HALF:] = res[4:8].astype(BF16)
    for i, out in ((0, out_in), (1, out_out)):
        out[...] = both_cores(0, i) + g_in(1, i, chip_peer[1]) + g_in(2, i, chip_peer[2])
    landed.wait_send()
    for copy in started:
        copy.wait_send()


def local(tokens, upstream, experts, gates, w_in, w_out):
    vmem = pl.BlockSpec(memory_space=pltpu.VMEM)

    def hbm(a):
        return pltpu.with_memory_space_constraint(a, pltpu.HBM)

    dma = pltpu.SemaphoreType.DMA
    width = 2 * HALF
    out_tok, out_in, out_out = pl.pallas_call(
        kernel,
        out_shape=(
            pltpu.VMEM((4, width), BF16),
            pltpu.VMEM((80, width), F32),
            pltpu.VMEM((80, width), F32),
        ),
        in_specs=[pl.BlockSpec(memory_space=pltpu.HBM)] * 6,
        out_specs=(vmem, vmem, vmem),
        scratch_shapes=[
            pltpu.VMEM((4, width), BF16),
            pltpu.VMEM((4, width), BF16),
            pltpu.VMEM((2, 64), jnp.int32),
            pltpu.VMEM((2, 64), F32),
            pltpu.VMEM((NE, 16, HALF), BF16),
            pltpu.VMEM((NY, 40, HALF), BF16),
            pltpu.VMEM((80, width), BF16),
            pltpu.VMEM((80, width), BF16),
            pltpu.VMEM((2 * NX, 80, width), BF16),
            pltpu.VMEM((2 * NX, 80, width), BF16),
            pltpu.VMEM((80, width), BF16),
            pltpu.VMEM((NY - 1, 24, HALF), BF16),
            pltpu.VMEM((NY - 1, 24, HALF), BF16),
            pltpu.VMEM((NE, 8, HALF), BF16),
            pltpu.VMEM((NE - 1, 8, HALF), BF16),
            pltpu.VMEM((2, 2 * NX, 80, width), BF16),
            pltpu.VMEM((2, NX, 80, width), BF16),
            pltpu.VMEM((NX - 1, 2, 80, width), BF16),
            pltpu.VMEM((NX - 1, 2, 80, width), BF16),
            dma((6,)), dma((NE,)), dma((NE,)), dma((2, 7)), dma((2, 2 * NX)), dma((NY,)), dma((NY,)),
            dma((NY - 1,)), dma((NY - 1,)), dma, dma, dma((2, NX)), dma((2, NX)),
            dma((NX - 1, 2)), dma((NX - 1, 2)),
        ],
        compiler_params=pltpu.CompilerParams(
            collective_id=0, has_side_effects=True, vmem_limit_bytes=56 * 1024 * 1024
        ),
        cost_estimate=pl.CostEstimate(flops=700_000_000, bytes_accessed=2_000_000, transcendentals=51200),
        name="moe_backward",
    )(*(hbm(a) for a in (tokens, upstream, experts.T, gates.T, w_in[0].T, w_out[0])))
    return out_tok, out_in.T[None], out_out[None]


def solution(mesh):
    in_specs = (
        P(("replica", "expert"), None),
        P(("replica", "expert"), None),
        P("replica", None),
        P("replica", None),
        P("expert", None, "replica"),
        P("expert", "replica", None),
    )
    out_specs = (
        P(("replica", "expert"), None),
        P("expert", None, "replica"),
        P("expert", "replica", None),
    )
    return jax.shard_map(local, mesh=mesh, in_specs=in_specs, out_specs=out_specs, check_vma=False)
```
